768 devices in a mesh: pair: 24 (over z, core), integ: 32 (over x, y).
Axes of the slice: x: 4, y: 8, z: 12, core: 2. Of those that a mesh axis runs over, the one named last changes fastest.
Arguments:
- amplitudes: bfloat16 [768, 32768], P('pair', 'integ'), may hold values from -6 to 6
- integrals: bfloat16 [32768, 12288], P('integ', 'pair'), may hold values from -0.03125 to 0.03125
- driver: bfloat16 [768, 12288], P(('pair', 'integ')), may hold values from -6 to 6
- occ_pairs: int32 [768, 2], P(('pair', 'integ')), may hold values from 0 to 99
- ab_tiles: int32 [3, 2], replicated, may hold values from 0 to 10
- eps_occ: float32 [100], replicated, may hold values from -3 to -0.3
- eps_vir: float32 [704], replicated, may hold values from 0.2 to 3
Outputs:
- residual: bfloat16 [768, 12288], P(('pair', 'integ'))
- increment: float32 [768, 12288], P(('pair', 'integ'))
The draws below stay inside these ranges and needn't reach their ends.
All inputs are finite; a program needn't handle non-finite values.
Results may differ from the reference program's by a relative error of at most 0.018.
Values may be sent and summed in bfloat16 or wider, within the bound.
No kernel may reach another device: no remote copies, remote signals or barrier semaphores. Data moves between devices by JAX's collectives and lax.ppermute only.
A program may use at most 32 MiB of HBM per device.

```python
import jax
import jax.numpy as jnp
from jax import lax

TW = 64
NV = 704
NO = 100
VT = 11
ABT = 3
OW = 768
CD = 32768
ABW = 12288
N_INTEG = 32


def plant(array, rng, least, high):
    shape = array.shape
    place = [jax.random.randint(jax.random.fold_in(rng, axis), (), 0, shape[axis]) for axis in range(len(shape))]
    array = array.at[tuple(place)].set(least)
    longest = shape.index(max(shape))
    place[longest] = (place[longest] + 1) % shape[longest]
    return array.at[tuple(place)].set(high)


def level_of(key, shape, pieces, smallest, high):
    loudness, own = 1.0, jax.random.fold_in(key, 6)
    for axis_at, shards_of in pieces:
        heights = jnp.exp(jax.random.uniform(jax.random.fold_in(own, axis_at), (shards_of,), jnp.float32, smallest / len(pieces), high / len(pieces)))
        loudness = loudness * jnp.repeat(heights, shape[axis_at] // shards_of).reshape([-1 if axis == axis_at else 1 for axis in range(len(shape))])
    return loudness


def bell_draw(own_key, extent, deviation, limit, split=(), kind=jnp.bfloat16):
    level = level_of(own_key, extent, split, -0.22, 0.18) if split else 1.0
    entries = jax.random.normal(own_key, extent, jnp.float32) * deviation * level
    return jnp.minimum(jnp.maximum(entries, -limit), limit).astype(kind)


def setup_inputs(seed: int = 0) -> dict:
    keys = jax.random.split(jax.random.key(seed), 8)
    return {
        "amplitudes": bell_draw(keys[0], (OW, CD), 1.0, 6.0, ((0, 24), (1, 32))),
        "integrals": bell_draw(keys[1], (CD, ABW), CD ** -0.5, 0.03125, ((0, 32), (1, 24))),
        "driver": bell_draw(keys[2], (OW, ABW), 1.0, 6.0, ((0, 768),)),
        "occ_pairs": plant(jax.random.randint(keys[3], (OW, 2), 0, NO), jax.random.fold_in(keys[3], 1), 0, NO - 1).astype(jnp.int32),
        "ab_tiles": plant(jax.random.randint(keys[4], (ABT, 2), 0, VT), jax.random.fold_in(keys[4], 1), 0, VT - 1).astype(jnp.int32),
        "eps_occ": jnp.clip(jax.random.uniform(keys[5], (NO,), jnp.float32, -3.0, -0.3), -3.0, -0.3),
        "eps_vir": jnp.clip(jax.random.uniform(keys[6], (NV,), jnp.float32, 0.2, 3.0), 0.2, 3.0),
    }


def denominators(occ_pairs, ab_tiles, eps_occ, eps_vir):
    column = jnp.arange(ABT * TW * TW, dtype=jnp.int32)
    tile_index = column // (TW * TW)
    first_vir = ab_tiles[tile_index, 0] * TW + (column // TW) % TW
    second_vir = ab_tiles[tile_index, 1] * TW + column % TW
    vir_sum = eps_vir[first_vir] + eps_vir[second_vir]
    occ_sum = eps_occ[occ_pairs[:, 0]] + eps_occ[occ_pairs[:, 1]]
    return vir_sum[None, :] - occ_sum[:, None]


def reference(amplitudes, integrals, driver, occ_pairs, ab_tiles, eps_occ, eps_vir):
    block_len = CD // N_INTEG

    def add_block(g, total):
        start = (g * block_len).astype(jnp.int32)
        left = lax.dynamic_slice_in_dim(amplitudes, start, block_len, 1)
        right = lax.dynamic_slice_in_dim(integrals, start, block_len, 0)
        part = jnp.dot(left, right, preferred_element_type=jnp.float32).astype(jnp.bfloat16)
        part = lax.optimization_barrier(part)
        return total + part.astype(jnp.float32)

    ladder = lax.fori_loop(jnp.int32(0), jnp.int32(N_INTEG), add_block, jnp.zeros((OW, ABW), jnp.float32))
    residual = (driver.astype(jnp.float32) + ladder).astype(jnp.bfloat16)
    increment = residual.astype(jnp.float32) / denominators(occ_pairs, ab_tiles, eps_occ, eps_vir)
    return residual, increment
```

```python
import jax
import jax.numpy as jnp
import numpy as np
from jax import lax
from jax.sharding import Mesh, PartitionSpec as P

TW = 64
NZ, NCORE, NX, NY = 12, 2, 4, 8


def denominators(occ_pairs, ab_tiles, eps_occ, eps_vir):
    blocks = []
    for tile_pair in range(ab_tiles.shape[0]):
        first_vir = lax.dynamic_slice_in_dim(eps_vir, ab_tiles[tile_pair, 0] * TW, TW)
        second_vir = lax.dynamic_slice_in_dim(eps_vir, ab_tiles[tile_pair, 1] * TW, TW)
        blocks.append((first_vir[:, None] + second_vir[None, :]).reshape(-1))
    vir_sum = jnp.concatenate(blocks)
    occ_sum = eps_occ[occ_pairs[:, 0]] + eps_occ[occ_pairs[:, 1]]
    return vir_sum[None, :] - occ_sum[:, None]


def per_device(amplitudes, integrals, driver, occ_pairs, ab_tiles, eps_occ, eps_vir):
    core = lax.axis_index("c")
    other = lax.ppermute(integrals, "c", [(0, 1), (1, 0)])
    rows = lax.all_gather(amplitudes, "z", axis=0, tiled=True)
    own_part = jnp.dot(rows, integrals, preferred_element_type=jnp.float32)
    other_part = jnp.dot(rows, other, preferred_element_type=jnp.float32)
    partial_value = jnp.concatenate([own_part, other_part], axis=1).astype(jnp.bfloat16)
    width = partial_value.shape[1]
    by_x = partial_value.reshape(NZ, NX, NY, width).transpose(1, 0, 2, 3).reshape(NX, NZ * NY, width)
    by_x = lax.all_to_all(by_x, "x", 0, 0)
    over_x = jnp.sum(by_x.astype(jnp.float32), axis=0).astype(jnp.bfloat16)
    by_zy = lax.all_to_all(over_x.reshape(NZ * NY, width // 128, 128), ("z", "y"), 0, 0)
    ladder = jnp.sum(by_zy.reshape(NZ, NY, width).astype(jnp.float32), axis=1)
    ladder = ladder.reshape(NZ, 2, width // 2)
    ladder = jnp.where(core == 0, ladder, ladder[:, ::-1]).reshape(1, -1)
    residual = (driver.astype(jnp.float32) + ladder).astype(jnp.bfloat16)
    increment = residual.astype(jnp.float32) / denominators(occ_pairs, ab_tiles, eps_occ, eps_vir)
    return (residual, increment)


def solution(mesh):
    devices = np.asarray(mesh.devices).reshape(NZ, NCORE, NX, NY)
    fine = Mesh(devices, ("z", "c", "x", "y"))
    pair, integ = ("z", "c"), ("x", "y")
    every = pair + integ
    placed = (P(pair, integ), P(integ, pair), P(every, None), P(every, None), P(), P(), P())
    return jax.shard_map(
        per_device,
        mesh=fine,
        in_specs=placed,
        out_specs=(P(every, None), P(every, None)),
        check_vma=False,
    )
```

```python
import jax
import jax.numpy as jnp
import numpy as np
from jax import lax
from jax.experimental import pallas as pl
from jax.experimental.pallas import tpu as pltpu
from jax.sharding import Mesh, PartitionSpec as P

TW = 64
LANES = 128
NZ, NCORE, NX, NYH, NYL = 12, 2, 4, 4, 2
VMEM_SPEC = pl.BlockSpec(memory_space=pltpu.VMEM)
SMEM_SPEC = pl.BlockSpec(memory_space=pltpu.SMEM)


def row_order():
    count = NZ * NX * NYH * NYL
    rows = np.arange(count).reshape(NZ, NX, NYH, NYL).transpose(1, 3, 0, 2).reshape(-1)
    return (rows[:, None] == np.arange(count)[None, :]).astype(np.float32)


def product_kernel(order_ref, rows_ref, own_ref, other_ref, out_ref):
    core = lax.axis_index("c")
    groups, share, _ = out_ref.shape
    width = own_ref.shape[1]
    rows = jnp.dot(order_ref[...], rows_ref[...], preferred_element_type=jnp.float32).astype(jnp.bfloat16)
    for panel_ref, place in ((own_ref, core), (other_ref, 1 - core)):
        part = jnp.dot(rows, panel_ref[...], preferred_element_type=jnp.float32)
        columns = pl.ds(pl.multiple_of(place * width, width), width)
        out_ref[:, :, columns] = part.astype(jnp.bfloat16).reshape(groups, share, width)


def finish_kernel(occ_pairs, ab_tiles, eps_occ, eps_vir_ref, parts_ref, driver_ref, residual_ref, increment_ref, flat, line):
    blocks = flat.shape[0] // 8
    tile_rows = TW * TW // LANES
    lane = lax.broadcasted_iota(jnp.int32, (1, LANES), 1)
    grid_lane = lax.broadcasted_iota(jnp.int32, (tile_rows, LANES), 1)
    grid_row = lax.broadcasted_iota(jnp.int32, (tile_rows, LANES), 0)

    def orbitals(tile):
        count = eps_vir_ref.shape[1]
        picked = jnp.zeros((1, LANES), jnp.float32)
        for start in range(0, count, LANES):
            size = min(LANES, count - start)
            piece = eps_vir_ref[0:1, start : start + size]
            if size < LANES:
                piece = jnp.concatenate([piece, jnp.zeros((1, LANES - size), jnp.float32)], axis=1)
            picked = jnp.where(tile // 2 == start // LANES, piece, picked)
        return jnp.where(tile % 2 == 1, pltpu.roll(picked, TW, 1), picked)

    occ_sum = eps_occ[occ_pairs[0, 0]] + eps_occ[occ_pairs[0, 1]]
    for column in range(driver_ref.shape[1] // LANES):
        flat[column : column + 1, :] = line_of(driver_ref, column).astype(jnp.float32)
    for tile_pair in range(ab_tiles.shape[1]):
        first = jnp.broadcast_to(orbitals(ab_tiles[0, tile_pair]), (tile_rows, LANES))
        second = orbitals(ab_tiles[1, tile_pair])
        second = jnp.where(lane < TW, second, pltpu.roll(second, TW, 1))
        even = jnp.sum(jnp.where(grid_lane == 2 * grid_row, first, 0.0), axis=1, keepdims=True)
        odd = jnp.sum(jnp.where(grid_lane == 2 * grid_row + 1, first, 0.0), axis=1, keepdims=True)
        denominator = jnp.where(grid_lane < TW, even, odd) + second - occ_sum
        for block in range(tile_rows // 8):
            at = tile_pair * (tile_rows // 8) + block
            ladder = parts_ref[at * NYH].astype(jnp.float32)
            for part in range(1, NYH):
                ladder = ladder + parts_ref[at * NYH + part].astype(jnp.float32)
            residual = (flat[at * 8 : at * 8 + 8, :] + ladder).astype(jnp.bfloat16).astype(jnp.float32)
            increment = residual / denominator[block * 8 : block * 8 + 8, :]
            for row in range(8):
                columns = slice((at * 8 + row) * LANES, (at * 8 + row + 1) * LANES)
                line[0:1, columns] = residual[row : row + 1, :]
                increment_ref[0:1, columns] = increment[row : row + 1, :]
    residual_ref[...] = line[...].astype(jnp.bfloat16)


def line_of(ref, column):
    return ref[0:1, column * LANES : (column + 1) * LANES]


def per_device(amplitudes, integrals, driver, occ_pairs, ab_tiles, eps_occ, eps_vir):
    other = lax.ppermute(integrals, "c", [(0, 1), (1, 0)])
    rows = lax.all_gather(amplitudes, "z", axis=0, tiled=True)
    width = NCORE * integrals.shape[1]
    share = rows.shape[0] // (NX * NYL)
    by_x = pl.pallas_call(
        product_kernel,
        out_shape=jax.ShapeDtypeStruct((NX * NYL, share, width), jnp.bfloat16),
        in_specs=[VMEM_SPEC] * 4,
        out_specs=VMEM_SPEC,
        compiler_params=pltpu.CompilerParams(vmem_limit_bytes=24 * 2**20),
        name="product",
    )(jnp.asarray(row_order(), jnp.bfloat16), rows, integrals, other)
    by_x = lax.all_to_all(by_x, ("x", "yl"), 0, 0)
    over_x = jnp.sum(by_x.astype(jnp.float32), axis=0).astype(jnp.bfloat16)
    by_z = lax.all_to_all(over_x.reshape(share, width // LANES, LANES), ("z", "yh"), 0, 0)
    columns = driver.shape[1]
    return pl.pallas_call(
        finish_kernel,
        out_shape=(
            jax.ShapeDtypeStruct((1, columns), jnp.bfloat16),
            jax.ShapeDtypeStruct((1, columns), jnp.float32),
        ),
        in_specs=[SMEM_SPEC] * 3 + [VMEM_SPEC] * 3,
        out_specs=(VMEM_SPEC, VMEM_SPEC),
        scratch_shapes=[
            pltpu.VMEM((columns // LANES, LANES), jnp.float32),
            pltpu.VMEM((1, columns), jnp.float32),
        ],
        compiler_params=pltpu.CompilerParams(vmem_limit_bytes=8 * 2**20),
        name="finish",
    )(occ_pairs, ab_tiles.T, eps_occ, eps_vir.reshape(1, -1), by_z, driver)


def solution(mesh):
    devices = np.asarray(mesh.devices).reshape(NZ, NCORE, NX, NYH, NYL)
    fine = Mesh(devices, ("z", "c", "x", "yh", "yl"))
    pair, integ = ("z", "c"), ("x", "yh", "yl")
    every = pair + integ
    placed = (P(pair, integ), P(integ, pair), P(every, None), P(every, None), P(), P(), P())
    return jax.shard_map(
        per_device,
        mesh=fine,
        in_specs=placed,
        out_specs=(P(every, None), P(every, None)),
        check_vma=False,
    )
```

```python
import jax
import jax.numpy as jnp
import numpy as np
from jax import lax
from jax.experimental import pallas as pl
from jax.experimental.pallas import tpu as pltpu
from jax.sharding import Mesh, PartitionSpec as P

TW = 64
LANES = 128
NZ, NCORE, NX, NYH, NYL = 12, 2, 4, 4, 2
VMEM_SPEC = pl.BlockSpec(memory_space=pltpu.VMEM)
SMEM_SPEC = pl.BlockSpec(memory_space=pltpu.SMEM)


def row_order():
    count = NZ * NX * NYH * NYL
    rows = np.arange(count).reshape(NZ, NX, NYH, NYL).transpose(1, 3, 0, 2).reshape(-1)
    return (rows[:, None] == np.arange(count)[None, :]).astype(np.float32)


def line_of(ref, column):
    return ref[0:1, column * LANES : (column + 1) * LANES]


def product_kernel(
    occ_pairs, ab_tiles, eps_occ, eps_vir_ref, driver_ref, order_ref, rows_ref, other_ref, own_hbm,
    out_ref, denominator_ref, wide_ref, own_ref, own_sem,
):
    own_copy = pltpu.make_async_copy(own_hbm, own_ref, own_sem)
    own_copy.start()
    core = lax.axis_index("c")
    groups, share, _ = out_ref.shape
    width = own_ref.shape[1]
    rows = rows_ref[...].reshape(groups * share, -1)
    rows = jnp.dot(order_ref[...], rows, preferred_element_type=jnp.float32).astype(jnp.bfloat16)

    def multiply(panel_ref, place):
        part = jnp.dot(rows, panel_ref[...], preferred_element_type=jnp.float32)
        columns = pl.ds(pl.multiple_of(place * width, width), width)
        out_ref[:, :, columns] = part.astype(jnp.bfloat16).reshape(groups, share, width)

    multiply(other_ref, 1 - core)
    own_copy.wait()
    multiply(own_ref, core)
    denominators(occ_pairs, ab_tiles, eps_occ, eps_vir_ref, denominator_ref)
    for column in range(driver_ref.shape[1] // LANES):
        wide_ref[column : column + 1, :] = line_of(driver_ref, column).astype(jnp.float32)


def denominators(occ_pairs, ab_tiles, eps_occ, eps_vir_ref, denominator_ref):
    tile_rows = TW * TW // LANES
    lane = lax.broadcasted_iota(jnp.int32, (1, LANES), 1)
    grid_lane = lax.broadcasted_iota(jnp.int32, (tile_rows, LANES), 1)
    grid_row = lax.broadcasted_iota(jnp.int32, (tile_rows, LANES), 0)

    def orbitals(tile):
        count = eps_vir_ref.shape[1]
        picked = jnp.zeros((1, LANES), jnp.float32)
        for start in range(0, count, LANES):
            size = min(LANES, count - start)
            piece = eps_vir_ref[0:1, start : start + size]
            if size < LANES:
                piece = jnp.concatenate([piece, jnp.zeros((1, LANES - size), jnp.float32)], axis=1)
            picked = jnp.where(tile // 2 == start // LANES, piece, picked)
        return jnp.where(tile % 2 == 1, pltpu.roll(picked, TW, 1), picked)

    occ_sum = eps_occ[occ_pairs[0, 0]] + eps_occ[occ_pairs[0, 1]]
    for tile_pair in range(ab_tiles.shape[1]):
        first = jnp.broadcast_to(orbitals(ab_tiles[0, tile_pair]), (tile_rows, LANES))
        second = orbitals(ab_tiles[1, tile_pair])
        second = jnp.where(lane < TW, second, pltpu.roll(second, TW, 1))
        even = jnp.sum(jnp.where(grid_lane == 2 * grid_row, first, 0.0), axis=1, keepdims=True)
        odd = jnp.sum(jnp.where(grid_lane == 2 * grid_row + 1, first, 0.0), axis=1, keepdims=True)
        rows = slice(tile_pair * tile_rows, (tile_pair + 1) * tile_rows)
        denominator_ref[rows, :] = jnp.where(grid_lane < TW, even, odd) + second - occ_sum


def finish_kernel(parts_ref, wide_ref, denominator_ref, residual_ref, increment_ref, line):
    for at in range(wide_ref.shape[0] // 8):
        ladder = parts_ref[at * NYH].astype(jnp.float32)
        for part in range(1, NYH):
            ladder = ladder + parts_ref[at * NYH + part].astype(jnp.float32)
        residual = (wide_ref[at * 8 : at * 8 + 8, :] + ladder).astype(jnp.bfloat16).astype(jnp.float32)
        increment = residual / denominator_ref[at * 8 : at * 8 + 8, :]
        for row in range(8):
            columns = slice((at * 8 + row) * LANES, (at * 8 + row + 1) * LANES)
            line[0:1, columns] = residual[row : row + 1, :]
            increment_ref[0:1, columns] = increment[row : row + 1, :]
    residual_ref[...] = line[...].astype(jnp.bfloat16)


def per_device(amplitudes, integrals, driver, occ_pairs, ab_tiles, eps_occ, eps_vir):
    other = lax.ppermute(integrals, "c", [(0, 1), (1, 0)])
    rows = lax.all_gather(lax.optimization_barrier(amplitudes[None]), "z", axis=0, tiled=True)
    width = NCORE * integrals.shape[1]
    share = NZ * NYH
    columns = driver.shape[1]
    shape = (columns // LANES, LANES)
    by_x, denominator, wide = pl.pallas_call(
        product_kernel,
        out_shape=(
            jax.ShapeDtypeStruct((NX * NYL, share, width), jnp.bfloat16),
            jax.ShapeDtypeStruct(shape, jnp.float32),
            jax.ShapeDtypeStruct(shape, jnp.float32),
        ),
        in_specs=[SMEM_SPEC] * 3 + [VMEM_SPEC] * 5 + [pl.BlockSpec(memory_space=pltpu.HBM)],
        out_specs=(VMEM_SPEC,) * 3,
        scratch_shapes=[pltpu.VMEM(integrals.shape, jnp.bfloat16), pltpu.SemaphoreType.DMA],
        compiler_params=pltpu.CompilerParams(vmem_limit_bytes=52 * 2**20),
        name="product",
    )(
        occ_pairs, ab_tiles.T, eps_occ, eps_vir.reshape(1, -1), driver,
        jnp.asarray(row_order(), jnp.bfloat16), rows, other, integrals,
    )
    by_x = lax.all_to_all(by_x, ("x", "yl"), 0, 0)
    over_x = jnp.sum(by_x.astype(jnp.float32), axis=0).astype(jnp.bfloat16)
    by_z = lax.all_to_all(over_x.reshape(share, width // LANES, LANES), ("z", "yh"), 0, 0)
    return pl.pallas_call(
        finish_kernel,
        out_shape=(
            jax.ShapeDtypeStruct((1, columns), jnp.bfloat16),
            jax.ShapeDtypeStruct((1, columns), jnp.float32),
        ),
        in_specs=[VMEM_SPEC] * 3,
        out_specs=(VMEM_SPEC, VMEM_SPEC),
        scratch_shapes=[pltpu.VMEM((1, columns), jnp.float32)],
        compiler_params=pltpu.CompilerParams(vmem_limit_bytes=8 * 2**20),
        name="finish",
    )(by_z, wide, denominator)


def solution(mesh):
    devices = np.asarray(mesh.devices).reshape(NZ, NCORE, NX, NYH, NYL)
    fine = Mesh(devices, ("z", "c", "x", "yh", "yl"))
    pair, integ = ("z", "c"), ("x", "yh", "yl")
    every = pair + integ
    placed = (P(pair, integ), P(integ, pair), P(every, None), P(every, None), P(), P(), P())
    return jax.shard_map(
        per_device,
        mesh=fine,
        in_specs=placed,
        out_specs=(P(every, None), P(every, None)),
        check_vma=False,
    )
```

```python
import jax
import jax.numpy as jnp
import numpy as np
from jax import lax
from jax.experimental import pallas as pl
from jax.experimental.pallas import tpu as pltpu
from jax.sharding import Mesh, PartitionSpec as P

TW = 64
LANES = 128
NZ, NCORE, NX, NYH, NYL = 12, 2, 4, 4, 2
VMEM_SPEC = pl.BlockSpec(memory_space=pltpu.VMEM)
SMEM_SPEC = pl.BlockSpec(memory_space=pltpu.SMEM)


NEAR = [((x + 2) % NX, yl) for x in range(NX) for yl in range(NYL)]
FAR = [((z + NZ // 2) % NZ, (yh + NYH // 2) % NYH) for z in range(NZ) for yh in range(NYH)]
NEAR_GROUP = [[x * NYL + yl for x, yl in NEAR]]
FAR_GROUP = [[z * NYH + yh for z, yh in FAR]]


def row_order():
    count = NZ * NX * NYH * NYL
    rows = np.array([((z * NX + x) * NYH + yh) * NYL + yl for x, yl in NEAR for z, yh in FAR])
    return (rows[:, None] == np.arange(count)[None, :]).astype(np.float32)


def line_of(ref, column):
    return ref[0:1, column * LANES : (column + 1) * LANES]


def product_kernel(
    occ_pairs, ab_tiles, eps_occ, eps_vir_ref, driver_ref, order_ref, rows_ref, other_ref, own_hbm,
    out_ref, denominator_ref, wide_ref, own_ref, own_sems,
):
    depth, width = own_ref.shape
    slab = depth // own_sems.shape[0]
    own_copies = [
        pltpu.make_async_copy(own_hbm.at[pl.ds(i * slab, slab)], own_ref.at[pl.ds(i * slab, slab)], own_sems.at[i])
        for i in range(own_sems.shape[0])
    ]
    for copy in own_copies:
        copy.start()
    core = lax.axis_index("c")
    groups, share, _ = out_ref.shape
    rows = rows_ref[...].reshape(groups * share, -1)
    rows = jnp.dot(order_ref[...], rows, preferred_element_type=jnp.float32).astype(jnp.bfloat16)

    def multiply(panel_ref, place):
        part = jnp.dot(rows, panel_ref[...], preferred_element_type=jnp.float32)
        columns = pl.ds(pl.multiple_of(place * width, width), width)
        out_ref[:, :, columns] = part.astype(jnp.bfloat16).reshape(groups, share, width)

    multiply(other_ref, 1 - core)
    denominators(occ_pairs, ab_tiles, eps_occ, eps_vir_ref, denominator_ref)
    for column in range(driver_ref.shape[1] // LANES):
        wide_ref[column : column + 1, :] = line_of(driver_ref, column).astype(jnp.float32)
    for copy in own_copies:
        copy.wait()
    multiply(own_ref, core)


def denominators(occ_pairs, ab_tiles, eps_occ, eps_vir_ref, denominator_ref):
    tile_rows = TW * TW // LANES
    lane = lax.broadcasted_iota(jnp.int32, (1, LANES), 1)
    grid_lane = lax.broadcasted_iota(jnp.int32, (tile_rows, LANES), 1)
    grid_row = lax.broadcasted_iota(jnp.int32, (tile_rows, LANES), 0)

    def orbitals(tile):
        count = eps_vir_ref.shape[0]
        picked = jnp.zeros((1, LANES), jnp.float32)
        for start in range(0, count, LANES):
            size = min(LANES, count - start)
            piece = eps_vir_ref[start : start + size].reshape(1, size)
            if size < LANES:
                piece = jnp.concatenate([piece, jnp.zeros((1, LANES - size), jnp.float32)], axis=1)
            picked = jnp.where(tile // 2 == start // LANES, piece, picked)
        return jnp.where(tile % 2 == 1, pltpu.roll(picked, TW, 1), picked)

    occ_sum = eps_occ[occ_pairs[0, 0]] + eps_occ[occ_pairs[0, 1]]
    for tile_pair in range(ab_tiles.shape[1]):
        first = jnp.broadcast_to(orbitals(ab_tiles[0, tile_pair]), (tile_rows, LANES))
        second = orbitals(ab_tiles[1, tile_pair])
        second = jnp.where(lane < TW, second, pltpu.roll(second, TW, 1))
        even = jnp.sum(jnp.where(grid_lane == 2 * grid_row, first, 0.0), axis=1, keepdims=True)
        odd = jnp.sum(jnp.where(grid_lane == 2 * grid_row + 1, first, 0.0), axis=1, keepdims=True)
        rows = slice(tile_pair * tile_rows, (tile_pair + 1) * tile_rows)
        denominator_ref[rows, :] = jnp.where(grid_lane < TW, even, odd) + second - occ_sum


def finish_kernel(parts_ref, wide_ref, denominator_ref, residual_ref, increment_ref, line):
    for at in range(wide_ref.shape[0] // 8):
        places = [place for place, (z, _) in enumerate(FAR) if z == at]
        ladder = sum(parts_ref[place].astype(jnp.float32) for place in places)
        residual = (wide_ref[at * 8 : at * 8 + 8, :] + ladder).astype(jnp.bfloat16).astype(jnp.float32)
        increment = residual / denominator_ref[at * 8 : at * 8 + 8, :]
        for row in range(8):
            columns = slice((at * 8 + row) * LANES, (at * 8 + row + 1) * LANES)
            line[0:1, columns] = residual[row : row + 1, :]
            increment_ref[0:1, columns] = increment[row : row + 1, :]
    residual_ref[...] = line[...].astype(jnp.bfloat16)


def per_device(amplitudes, integrals, driver, occ_pairs, ab_tiles, eps_occ, eps_vir):
    other = lax.ppermute(integrals, "c", [(0, 1), (1, 0)])
    rows = lax.all_gather(lax.optimization_barrier(amplitudes[None]), "z", axis=0, tiled=True)
    width = NCORE * integrals.shape[1]
    share = NZ * NYH
    columns = driver.shape[1]
    shape = (columns // LANES, LANES)
    by_x, denominator, wide = pl.pallas_call(
        product_kernel,
        out_shape=(
            jax.ShapeDtypeStruct((NX * NYL, share, width), jnp.bfloat16),
            jax.ShapeDtypeStruct(shape, jnp.float32),
            jax.ShapeDtypeStruct(shape, jnp.float32),
        ),
        in_specs=[SMEM_SPEC] * 3 + [VMEM_SPEC] * 5 + [pl.BlockSpec(memory_space=pl.ANY)],
        out_specs=(VMEM_SPEC,) * 3,
        scratch_shapes=[pltpu.VMEM(integrals.shape, jnp.bfloat16), pltpu.SemaphoreType.DMA((8,))],
        compiler_params=pltpu.CompilerParams(vmem_limit_bytes=51 * 2**20),
        name="product",
    )(
        occ_pairs, ab_tiles.T, eps_occ, eps_vir, driver,
        jnp.asarray(row_order(), jnp.bfloat16), rows, other, integrals,
    )
    by_x = lax.all_to_all(by_x, ("x", "yl"), 0, 0, axis_index_groups=NEAR_GROUP)
    over_x = jnp.sum(by_x.astype(jnp.float32), axis=0).astype(jnp.bfloat16)
    by_z = lax.all_to_all(
        over_x.reshape(share, width // LANES, LANES), ("z", "yh"), 0, 0, axis_index_groups=FAR_GROUP
    )
    return pl.pallas_call(
        finish_kernel,
        out_shape=(
            jax.ShapeDtypeStruct((1, columns), jnp.bfloat16),
            jax.ShapeDtypeStruct((1, columns), jnp.float32),
        ),
        in_specs=[VMEM_SPEC] * 3,
        out_specs=(VMEM_SPEC, VMEM_SPEC),
        scratch_shapes=[pltpu.VMEM((1, columns), jnp.float32)],
        compiler_params=pltpu.CompilerParams(vmem_limit_bytes=8 * 2**20),
        name="finish",
    )(by_z, wide, denominator)


def solution(mesh):
    devices = np.asarray(mesh.devices).reshape(NZ, NCORE, NX, NYH, NYL)
    fine = Mesh(devices, ("z", "c", "x", "yh", "yl"))
    pair, integ = ("z", "c"), ("x", "yh", "yl")
    every = pair + integ
    placed = (P(pair, integ), P(integ, pair), P(every, None), P(every, None), P(), P(), P())
    return jax.shard_map(
        per_device,
        mesh=fine,
        in_specs=placed,
        out_specs=(P(every, None), P(every, None)),
        check_vma=False,
    )
```

```python
import jax
import jax.numpy as jnp
import numpy as np
from jax import lax
from jax.experimental import pallas as pl
from jax.experimental.pallas import tpu as pltpu
from jax.sharding import Mesh, PartitionSpec as P

TW = 64
LANES = 128
NZ, NCORE, NX, NYH, NYL = 12, 2, 4, 4, 2
VMEM_SPEC = pl.BlockSpec(memory_space=pltpu.VMEM)


NEAR = [((x + 2) % NX, yl) for x in range(NX) for yl in range(NYL)]
FAR = [((z + NZ // 2) % NZ, (yh + NYH // 2) % NYH) for z in range(NZ) for yh in range(NYH)]
NEAR_GROUP = [[x * NYL + yl for x, yl in NEAR]]
TURN = [[z * NCORE + (z + turn) % NCORE for z in range(NZ)] for turn in range(NCORE)]
FAR_GROUPS = [[turn[z] * NYH + yh for z, yh in FAR] for turn in TURN]


def row_order():
    count = NZ * NX * NYH * NYL
    rows = np.array([((z * NX + x) * NYH + yh) * NYL + yl for x, yl in NEAR for z, yh in FAR])
    return (rows[:, None] == np.arange(count)[None, :]).astype(np.float32)


def line_of(ref, column):
    return ref[0:1, column * LANES : (column + 1) * LANES]


def product_kernel(order_ref, rows_ref, other_ref, own_hbm, out_ref, own_ref, own_sem):
    own_copy = pltpu.make_async_copy(own_hbm, own_ref, own_sem)
    own_copy.start()
    core = lax.axis_index("c")
    groups, share, _ = out_ref.shape
    width = own_ref.shape[1]
    rows = rows_ref[...].reshape(groups * share, -1)
    rows = jnp.dot(order_ref[...], rows, preferred_element_type=jnp.float32).astype(jnp.bfloat16)

    def multiply(panel_ref, place):
        part = jnp.dot(rows, panel_ref[...], preferred_element_type=jnp.float32)
        columns = pl.ds(pl.multiple_of(place * width, width), width)
        out_ref[:, :, columns] = part.astype(jnp.bfloat16).reshape(groups, share, width)

    multiply(other_ref, 1 - core)
    own_copy.wait()
    multiply(own_ref, core)


def full_line(ref, start):
    size = min(LANES, ref.shape[0] - start)
    line = ref[start : start + size].reshape(1, size)
    if size == LANES:
        return line
    return jnp.concatenate([line, jnp.zeros((1, LANES - size), line.dtype)], axis=1)


def denominators(occ_ref, tiles_ref, eps_occ_ref, eps_vir_ref):
    tile_rows = TW * TW // LANES
    lane = lax.broadcasted_iota(jnp.int32, (1, LANES), 1)
    grid_lane = lax.broadcasted_iota(jnp.int32, (tile_rows, LANES), 1)
    grid_row = lax.broadcasted_iota(jnp.int32, (tile_rows, LANES), 0)
    lines = [full_line(eps_vir_ref, start) for start in range(0, eps_vir_ref.shape[0], LANES)]
    occ_line = full_line(eps_occ_ref, 0)

    def orbitals(tile):
        tile = jnp.broadcast_to(tile, (1, LANES))
        picked = lines[0]
        for at in range(1, len(lines)):
            picked = jnp.where(tile >> 1 == at, lines[at], picked)
        return jnp.where(tile & 1 == 1, pltpu.roll(picked, TW, 1), picked)

    def occupied(orbital):
        return jnp.sum(jnp.where(lane == orbital, occ_line, 0.0), axis=1, keepdims=True)

    occ_sum = occupied(occ_ref[0:1, 0:1]) + occupied(occ_ref[0:1, 1:2])
    blocks = []
    for pair in range(tiles_ref.shape[1]):
        first = jnp.broadcast_to(orbitals(tiles_ref[0:1, pair : pair + 1]), (tile_rows, LANES))
        second = orbitals(tiles_ref[1:2, pair : pair + 1])
        second = jnp.where(lane < TW, second, pltpu.roll(second, TW, 1))
        even = jnp.sum(jnp.where(grid_lane == 2 * grid_row, first, 0.0), axis=1, keepdims=True)
        odd = jnp.sum(jnp.where(grid_lane == 2 * grid_row + 1, first, 0.0), axis=1, keepdims=True)
        blocks.append(jnp.where(grid_lane < TW, even, odd) + second - occ_sum)
    return blocks


def finish_kernel(
    occ_ref, tiles_ref, eps_occ_ref, eps_vir_ref, driver_ref, parts_ref, residual_ref, increment_ref, wide, line
):
    for column in range(driver_ref.shape[1] // LANES):
        wide[column : column + 1, :] = line_of(driver_ref, column).astype(jnp.float32)
    denominator = jnp.concatenate(denominators(occ_ref, tiles_ref, eps_occ_ref, eps_vir_ref), axis=0)
    for at in range(wide.shape[0] // 8):
        places = [place for place, (z, _) in enumerate(FAR) if z == at]
        ladder = sum(parts_ref[place].astype(jnp.float32) for place in places)
        residual = (wide[at * 8 : at * 8 + 8, :] + ladder).astype(jnp.bfloat16).astype(jnp.float32)
        increment = residual / denominator[at * 8 : at * 8 + 8, :]
        for row in range(8):
            columns = slice((at * 8 + row) * LANES, (at * 8 + row + 1) * LANES)
            line[0:1, columns] = residual[row : row + 1, :]
            increment_ref[0:1, columns] = increment[row : row + 1, :]
    residual_ref[...] = line[...].astype(jnp.bfloat16)


def per_device(amplitudes, integrals, driver, occ_pairs, ab_tiles, eps_occ, eps_vir):
    other = lax.ppermute(integrals, "c", [(0, 1), (1, 0)])
    rows = lax.all_gather(
        lax.optimization_barrier(amplitudes[None]), ("z", "c"), axis=0, tiled=True, axis_index_groups=TURN
    )
    width = NCORE * integrals.shape[1]
    share = NZ * NYH
    columns = driver.shape[1]
    by_x = pl.pallas_call(
        product_kernel,
        out_shape=jax.ShapeDtypeStruct((NX * NYL, share, width), jnp.bfloat16),
        in_specs=[VMEM_SPEC] * 3 + [pl.BlockSpec(memory_space=pl.ANY)],
        out_specs=VMEM_SPEC,
        scratch_shapes=[pltpu.VMEM(integrals.shape, jnp.bfloat16), pltpu.SemaphoreType.DMA],
        compiler_params=pltpu.CompilerParams(vmem_limit_bytes=51 * 2**20),
        name="product",
    )(jnp.asarray(row_order(), jnp.bfloat16), rows, other, integrals)
    by_x = lax.all_to_all(by_x, ("x", "yl"), 0, 0, axis_index_groups=NEAR_GROUP)
    over_x = jnp.sum(by_x.astype(jnp.float32), axis=0).astype(jnp.bfloat16)
    by_z = lax.all_to_all(
        over_x.reshape(share, width // LANES, LANES), ("z", "c", "yh"), 0, 0, axis_index_groups=FAR_GROUPS
    )
    return pl.pallas_call(
        finish_kernel,
        out_shape=(
            jax.ShapeDtypeStruct((1, columns), jnp.bfloat16),
            jax.ShapeDtypeStruct((1, columns), jnp.float32),
        ),
        in_specs=[VMEM_SPEC] * 6,
        out_specs=(VMEM_SPEC, VMEM_SPEC),
        scratch_shapes=[
            pltpu.VMEM((columns // LANES, LANES), jnp.float32),
            pltpu.VMEM((1, columns), jnp.float32),
        ],
        compiler_params=pltpu.CompilerParams(vmem_limit_bytes=8 * 2**20),
        name="finish",
    )(occ_pairs, ab_tiles.T, eps_occ, eps_vir, driver, by_z)


def solution(mesh):
    devices = np.asarray(mesh.devices).reshape(NZ, NCORE, NX, NYH, NYL)
    fine = Mesh(devices, ("z", "c", "x", "yh", "yl"))
    pair, integ = ("z", "c"), ("x", "yh", "yl")
    every = pair + integ
    placed = (P(pair, integ), P(integ, pair), P(every, None), P(every, None), P(), P(), P())
    return jax.shard_map(
        per_device,
        mesh=fine,
        in_specs=placed,
        out_specs=(P(every, None), P(every, None)),
        check_vma=False,
    )
```

```python
import jax
import jax.numpy as jnp
import numpy as np
from jax import lax
from jax.experimental import pallas as pl
from jax.experimental.pallas import tpu as pltpu
from jax.sharding import Mesh, PartitionSpec as P

TW = 64
LANES = 128
NZ, NCORE, NX, NYH, NYL = 12, 2, 4, 4, 2
VMEM_SPEC = pl.BlockSpec(memory_space=pltpu.VMEM)


NEAR = [((x + 2) % NX, yl) for x in range(NX) for yl in range(NYL)]
FAR = [((z + NZ // 2) % NZ, (yh + NYH // 2) % NYH) for z in range(NZ) for yh in range(NYH)]
NEAR_GROUP = [[x * NYL + yl for x, yl in NEAR]]
FAR_GROUP = [[z * NYH + yh for z, yh in FAR]]


def row_order():
    count = NZ * NX * NYH * NYL
    rows = np.array([((z * NX + x) * NYH + yh) * NYL + yl for x, yl in NEAR for z, yh in FAR])
    return (rows[:, None] == np.arange(count)[None, :]).astype(np.float32)


def line_of(ref, column):
    return ref[0:1, column * LANES : (column + 1) * LANES]


def product_kernel(
    eps_occ_ref, order_ref, rows_ref, other_ref, own_hbm, occ_hbm, tiles_hbm,
    out_ref, scalars_ref, own_ref, occ_ref, tiles_ref, sems,
):
    occ_copy = pltpu.make_async_copy(occ_hbm, occ_ref, sems.at[0])
    tiles_copy = pltpu.make_async_copy(tiles_hbm, tiles_ref, sems.at[1])
    own_copy = pltpu.make_async_copy(own_hbm, own_ref, sems.at[2])
    for copy in (occ_copy, tiles_copy, own_copy):
        copy.start()
    core = lax.axis_index("c")
    groups, share, _ = out_ref.shape
    width = own_ref.shape[1]
    rows = rows_ref[...].reshape(groups * share, -1)
    rows = jnp.dot(order_ref[...], rows, preferred_element_type=jnp.float32).astype(jnp.bfloat16)

    def multiply(panel_ref, place):
        part = jnp.dot(rows, panel_ref[...], preferred_element_type=jnp.float32)
        columns = pl.ds(pl.multiple_of(place * width, width), width)
        out_ref[:, :, columns] = part.astype(jnp.bfloat16).reshape(groups, share, width)

    multiply(other_ref, 1 - core)
    occ_copy.wait()
    tiles_copy.wait()
    row_scalars(occ_ref, tiles_ref, eps_occ_ref, scalars_ref)
    own_copy.wait()
    multiply(own_ref, core)


def full_line(ref, start):
    size = min(LANES, ref.shape[0] - start)
    line = ref[start : start + size].reshape(1, size)
    if size == LANES:
        return line
    return jnp.concatenate([line, jnp.zeros((1, LANES - size), line.dtype)], axis=1)


def row_scalars(occ_ref, tiles_ref, eps_occ_ref, scalars_ref):
    lane = lax.broadcasted_iota(jnp.int32, (1, LANES), 1)
    occ_line = full_line(eps_occ_ref, 0)

    def occupied(orbital):
        return jnp.sum(jnp.where(lane == orbital, occ_line, 0.0), axis=1, keepdims=True)

    occ_sum = occupied(occ_ref[0:1, 0:1]) + occupied(occ_ref[0:1, 1:2])
    scalars_ref[0:1, :] = jnp.broadcast_to(occ_sum, (1, LANES))
    for pair in range(tiles_ref.shape[1]):
        for which in range(2):
            tile = tiles_ref[which : which + 1, pair : pair + 1].astype(jnp.float32)
            at = 1 + 2 * pair + which
            scalars_ref[at : at + 1, :] = jnp.broadcast_to(tile, (1, LANES))


def denominators(scalars_ref, eps_vir_ref, tile_pairs):
    tile_rows = TW * TW // LANES
    lane = lax.broadcasted_iota(jnp.int32, (1, LANES), 1)
    grid_lane = lax.broadcasted_iota(jnp.int32, (tile_rows, LANES), 1)
    grid_row = lax.broadcasted_iota(jnp.int32, (tile_rows, LANES), 0)
    lines = [full_line(eps_vir_ref, start) for start in range(0, eps_vir_ref.shape[0], LANES)]

    def orbitals(at):
        tile = scalars_ref[at : at + 1, :].astype(jnp.int32)
        picked = lines[0]
        for at in range(1, len(lines)):
            picked = jnp.where(tile >> 1 == at, lines[at], picked)
        return jnp.where(tile & 1 == 1, pltpu.roll(picked, TW, 1), picked)

    occ_sum = scalars_ref[0:1, :]
    blocks = []
    for pair in range(tile_pairs):
        first = jnp.broadcast_to(orbitals(1 + 2 * pair), (tile_rows, LANES))
        second = orbitals(2 + 2 * pair)
        second = jnp.where(lane < TW, second, pltpu.roll(second, TW, 1))
        even = jnp.sum(jnp.where(grid_lane == 2 * grid_row, first, 0.0), axis=1, keepdims=True)
        odd = jnp.sum(jnp.where(grid_lane == 2 * grid_row + 1, first, 0.0), axis=1, keepdims=True)
        blocks.append(jnp.where(grid_lane < TW, even, odd) + second - occ_sum)
    return blocks


def finish_kernel(scalars_ref, eps_vir_ref, driver_ref, parts_ref, residual_ref, increment_ref, wide, line):
    for column in range(driver_ref.shape[1] // LANES):
        wide[column : column + 1, :] = line_of(driver_ref, column).astype(jnp.float32)
    denominator = jnp.concatenate(denominators(scalars_ref, eps_vir_ref, wide.shape[0] * LANES // TW**2), axis=0)
    for at in range(wide.shape[0] // 8):
        places = [place for place, (z, _) in enumerate(FAR) if z == at]
        ladder = sum(parts_ref[place].astype(jnp.float32) for place in places)
        residual = (wide[at * 8 : at * 8 + 8, :] + ladder).astype(jnp.bfloat16).astype(jnp.float32)
        increment = residual / denominator[at * 8 : at * 8 + 8, :]
        for row in range(8):
            columns = slice((at * 8 + row) * LANES, (at * 8 + row + 1) * LANES)
            line[0:1, columns] = residual[row : row + 1, :]
            increment_ref[0:1, columns] = increment[row : row + 1, :]
    residual_ref[...] = line[...].astype(jnp.bfloat16)


def per_device(amplitudes, integrals, driver, occ_pairs, ab_tiles, eps_occ, eps_vir):
    other = lax.ppermute(integrals, "c", [(0, 1), (1, 0)])
    rows = lax.all_gather(lax.optimization_barrier(amplitudes[None]), "z", axis=0, tiled=True)
    width = NCORE * integrals.shape[1]
    share = NZ * NYH
    columns = driver.shape[1]
    by_x, scalars = pl.pallas_call(
        product_kernel,
        out_shape=(
            jax.ShapeDtypeStruct((NX * NYL, share, width), jnp.bfloat16),
            jax.ShapeDtypeStruct((8, LANES), jnp.float32),
        ),
        in_specs=[VMEM_SPEC] * 4 + [pl.BlockSpec(memory_space=pl.ANY)] * 3,
        out_specs=(VMEM_SPEC, VMEM_SPEC),
        scratch_shapes=[
            pltpu.VMEM(integrals.shape, jnp.bfloat16),
            pltpu.VMEM(occ_pairs.shape, jnp.int32),
            pltpu.VMEM(ab_tiles.shape[::-1], jnp.int32),
            pltpu.SemaphoreType.DMA((3,)),
        ],
        compiler_params=pltpu.CompilerParams(vmem_limit_bytes=51 * 2**20),
        name="product",
    )(eps_occ, jnp.asarray(row_order(), jnp.bfloat16), rows, other, integrals, occ_pairs, ab_tiles.T)
    by_x = lax.all_to_all(by_x, ("x", "yl"), 0, 0, axis_index_groups=NEAR_GROUP)
    over_x = jnp.sum(by_x.astype(jnp.float32), axis=0).astype(jnp.bfloat16)
    by_z = lax.all_to_all(
        over_x.reshape(share, width // LANES, LANES), ("z", "yh"), 0, 0, axis_index_groups=FAR_GROUP
    )
    return pl.pallas_call(
        finish_kernel,
        out_shape=(
            jax.ShapeDtypeStruct((1, columns), jnp.bfloat16),
            jax.ShapeDtypeStruct((1, columns), jnp.float32),
        ),
        in_specs=[VMEM_SPEC] * 4,
        out_specs=(VMEM_SPEC, VMEM_SPEC),
        scratch_shapes=[
            pltpu.VMEM((columns // LANES, LANES), jnp.float32),
            pltpu.VMEM((1, columns), jnp.float32),
        ],
        compiler_params=pltpu.CompilerParams(vmem_limit_bytes=8 * 2**20),
        name="finish",
    )(scalars, eps_vir, driver, by_z)


def solution(mesh):
    devices = np.asarray(mesh.devices).reshape(NZ, NCORE, NX, NYH, NYL)
    fine = Mesh(devices, ("z", "c", "x", "yh", "yl"))
    pair, integ = ("z", "c"), ("x", "yh", "yl")
    every = pair + integ
    placed = (P(pair, integ), P(integ, pair), P(every, None), P(every, None), P(), P(), P())
    return jax.shard_map(
        per_device,
        mesh=fine,
        in_specs=placed,
        out_specs=(P(every, None), P(every, None)),
        check_vma=False,
    )
```

```python
import jax
import jax.numpy as jnp
import numpy as np
from jax import lax
from jax.experimental import pallas as pl
from jax.experimental.pallas import tpu as pltpu
from jax.sharding import Mesh, PartitionSpec as P

TW = 64
LANES = 128
NZ, NCORE, NX, NYH, NYL = 12, 2, 4, 4, 2
VMEM_SPEC = pl.BlockSpec(memory_space=pltpu.VMEM)


NEAR = [((x + 2) % NX, yl) for x in range(NX) for yl in range(NYL)]
FAR = [((z + NZ // 2) % NZ, (yh + NYH // 2) % NYH) for z in range(NZ) for yh in range(NYH)]
NEAR_GROUP = [[x * NYL + yl for x, yl in NEAR]]
FAR_GROUP = [[z * NYH + yh for z, yh in FAR]]


def row_order():
    count = NZ * NX * NYH * NYL
    rows = np.array([((z * NX + x) * NYH + yh) * NYL + yl for x, yl in NEAR for z, yh in FAR])
    return (rows[:, None] == np.arange(count)[None, :]).astype(np.float32)


def line_of(ref, column):
    return ref[0:1, column * LANES : (column + 1) * LANES]


def product_kernel(
    eps_occ_ref, order_ref, rows_ref, other_ref, own_hbm, occ_hbm, tiles_hbm,
    out_ref, scalars_ref, own_ref, occ_ref, tiles_ref, sems,
):
    occ_copy = pltpu.make_async_copy(occ_hbm, occ_ref, sems.at[0])
    tiles_copy = pltpu.make_async_copy(tiles_hbm, tiles_ref, sems.at[1])
    own_copy = pltpu.make_async_copy(own_hbm, own_ref, sems.at[2])
    for copy in (occ_copy, tiles_copy, own_copy):
        copy.start()
    core = lax.axis_index("c")
    groups, share, _ = out_ref.shape
    width = own_ref.shape[1]
    rows = rows_ref[...].reshape(groups * share, -1)
    rows = jnp.dot(order_ref[...], rows, preferred_element_type=jnp.float32).astype(jnp.bfloat16)

    def multiply(panel_ref, place):
        part = jnp.dot(rows, panel_ref[...], preferred_element_type=jnp.float32)
        columns = pl.ds(pl.multiple_of(place * width, width), width)
        out_ref[:, :, columns] = part.astype(jnp.bfloat16).reshape(groups, share, width)

    multiply(other_ref, 1 - core)
    occ_copy.wait()
    tiles_copy.wait()
    row_scalars(occ_ref, tiles_ref, eps_occ_ref, scalars_ref)
    own_copy.wait()
    multiply(own_ref, core)


def full_line(ref, start):
    size = min(LANES, ref.shape[0] - start)
    line = ref[start : start + size].reshape(1, size)
    if size == LANES:
        return line
    return jnp.concatenate([line, jnp.zeros((1, LANES - size), line.dtype)], axis=1)


def row_scalars(occ_ref, tiles_ref, eps_occ_ref, scalars_ref):
    lane = lax.broadcasted_iota(jnp.int32, (1, LANES), 1)
    occ_line = full_line(eps_occ_ref, 0)

    def occupied(orbital):
        return jnp.sum(jnp.where(lane == orbital, occ_line, 0.0), axis=1, keepdims=True)

    occ_sum = occupied(occ_ref[0:1, 0:1]) + occupied(occ_ref[0:1, 1:2])
    scalars_ref[0:1, :] = jnp.broadcast_to(occ_sum, (1, LANES))
    for pair in range(tiles_ref.shape[0]):
        for which in range(2):
            tile = tiles_ref[pair : pair + 1, which : which + 1].astype(jnp.float32)
            at = 1 + 2 * pair + which
            scalars_ref[at : at + 1, :] = jnp.broadcast_to(tile, (1, LANES))


def denominators(scalars_ref, eps_vir_ref, tile_pairs):
    tile_rows = TW * TW // LANES
    lane = lax.broadcasted_iota(jnp.int32, (1, LANES), 1)
    grid_lane = lax.broadcasted_iota(jnp.int32, (tile_rows, LANES), 1)
    grid_row = lax.broadcasted_iota(jnp.int32, (tile_rows, LANES), 0)
    lines = [full_line(eps_vir_ref, start) for start in range(0, eps_vir_ref.shape[0], LANES)]

    def orbitals(at):
        tile = scalars_ref[at : at + 1, :].astype(jnp.int32)
        picked = lines[0]
        for at in range(1, len(lines)):
            picked = jnp.where(tile >> 1 == at, lines[at], picked)
        return jnp.where(tile & 1 == 1, pltpu.roll(picked, TW, 1), picked)

    occ_sum = scalars_ref[0:1, :]
    blocks = []
    for pair in range(tile_pairs):
        first = jnp.broadcast_to(orbitals(1 + 2 * pair), (tile_rows, LANES))
        second = orbitals(2 + 2 * pair)
        second = jnp.where(lane < TW, second, pltpu.roll(second, TW, 1))
        even = jnp.sum(jnp.where(grid_lane == 2 * grid_row, first, 0.0), axis=1, keepdims=True)
        odd = jnp.sum(jnp.where(grid_lane == 2 * grid_row + 1, first, 0.0), axis=1, keepdims=True)
        blocks.append(jnp.where(grid_lane < TW, even, odd) + second - occ_sum)
    return blocks


def finish_kernel(scalars_ref, eps_vir_ref, driver_ref, parts_ref, residual_ref, increment_ref, wide, line):
    for column in range(driver_ref.shape[1] // LANES):
        wide[column : column + 1, :] = line_of(driver_ref, column).astype(jnp.float32)
    denominator = jnp.concatenate(denominators(scalars_ref, eps_vir_ref, wide.shape[0] * LANES // TW**2), axis=0)
    for at in range(wide.shape[0] // 8):
        places = [place for place, (z, _) in enumerate(FAR) if z == at]
        ladder = sum(parts_ref[place].astype(jnp.float32) for place in places)
        residual = (wide[at * 8 : at * 8 + 8, :] + ladder).astype(jnp.bfloat16).astype(jnp.float32)
        increment = residual / denominator[at * 8 : at * 8 + 8, :]
        for row in range(8):
            columns = slice((at * 8 + row) * LANES, (at * 8 + row + 1) * LANES)
            line[0:1, columns] = residual[row : row + 1, :]
            increment_ref[0:1, columns] = increment[row : row + 1, :]
    residual_ref[...] = line[...].astype(jnp.bfloat16)


def per_device(amplitudes, integrals, driver, occ_pairs, ab_tiles, eps_occ, eps_vir):
    other = lax.ppermute(integrals, "c", [(0, 1), (1, 0)])
    rows = lax.all_gather(lax.optimization_barrier(amplitudes[None]), "z", axis=0, tiled=True)
    width = NCORE * integrals.shape[1]
    share = NZ * NYH
    columns = driver.shape[1]
    by_x, scalars = pl.pallas_call(
        product_kernel,
        out_shape=(
            jax.ShapeDtypeStruct((NX * NYL, share, width), jnp.bfloat16),
            jax.ShapeDtypeStruct((8, LANES), jnp.float32),
        ),
        in_specs=[VMEM_SPEC] * 4 + [pl.BlockSpec(memory_space=pl.ANY)] * 3,
        out_specs=(VMEM_SPEC, VMEM_SPEC),
        scratch_shapes=[
            pltpu.VMEM(integrals.shape, jnp.bfloat16),
            pltpu.VMEM(occ_pairs.shape, jnp.int32),
            pltpu.VMEM(ab_tiles.shape, jnp.int32),
            pltpu.SemaphoreType.DMA((3,)),
        ],
        compiler_params=pltpu.CompilerParams(vmem_limit_bytes=51 * 2**20),
        name="product",
    )(eps_occ, jnp.asarray(row_order(), jnp.bfloat16), rows, other, integrals, occ_pairs, ab_tiles)
    by_x = lax.all_to_all(by_x, ("x", "yl"), 0, 0, axis_index_groups=NEAR_GROUP)
    over_x = jnp.sum(by_x.astype(jnp.float32), axis=0).astype(jnp.bfloat16)
    by_z = lax.all_to_all(
        over_x.reshape(share, width // LANES, LANES), ("z", "yh"), 0, 0, axis_index_groups=FAR_GROUP
    )
    return pl.pallas_call(
        finish_kernel,
        out_shape=(
            jax.ShapeDtypeStruct((1, columns), jnp.bfloat16),
            jax.ShapeDtypeStruct((1, columns), jnp.float32),
        ),
        in_specs=[VMEM_SPEC] * 4,
        out_specs=(VMEM_SPEC, VMEM_SPEC),
        scratch_shapes=[
            pltpu.VMEM((columns // LANES, LANES), jnp.float32),
            pltpu.VMEM((1, columns), jnp.float32),
        ],
        compiler_params=pltpu.CompilerParams(vmem_limit_bytes=8 * 2**20),
        name="finish",
    )(scalars, eps_vir, driver, by_z)


def solution(mesh):
    devices = np.asarray(mesh.devices).reshape(NZ, NCORE, NX, NYH, NYL)
    fine = Mesh(devices, ("z", "c", "x", "yh", "yl"))
    pair, integ = ("z", "c"), ("x", "yh", "yl")
    every = pair + integ
    placed = (P(pair, integ), P(integ, pair), P(every, None), P(every, None), P(), P(), P())
    return jax.shard_map(
        per_device,
        mesh=fine,
        in_specs=placed,
        out_specs=(P(every, None), P(every, None)),
        check_vma=False,
    )
```

```python
import jax
import jax.numpy as jnp
import numpy as np
from jax import lax
from jax.experimental import pallas as pl
from jax.experimental.pallas import tpu as pltpu
from jax.sharding import Mesh, PartitionSpec as P

TW = 64
LANES = 128
NZ, NCORE, NX, NYH, NYL = 12, 2, 4, 4, 2
VMEM_SPEC = pl.BlockSpec(memory_space=pltpu.VMEM)


NY = NYH * NYL


def late_first(count):
    return [(at + count // 2) % count for at in range(count)]


LATE_Z, LATE_X, LATE_Y = late_first(NZ), late_first(NX), late_first(NY)
NEAR = (
    [[(x, y + yl) for x in LATE_X for yl in range(NYL)] for y in range(0, NY, NYL)],
    [[(x, y) for y in LATE_Y] for x in range(NX)],
)
FAR = (
    [[(z, x, y + yl) for z in LATE_Z for y in LATE_Y[::NYL]] for x in range(NX) for yl in range(NYL)],
    [[(z, x, y) for z in LATE_Z for x in LATE_X] for y in range(NY)],
)
NEAR_GROUPS = [[(core * NX + x) * NY + y for x, y in group] for core in range(NCORE) for group in NEAR[core]]
FAR_GROUPS = [[((z * NCORE + core) * NX + x) * NY + y for z, x, y in group] for core in range(NCORE) for group in FAR[core]]


def row_order(core):
    if core == 0:
        sent = [(z, x, y + yl) for x, yl in NEAR[0][0] for z in LATE_Z for y in LATE_Y[::NYL]]
    else:
        sent = [(z, x, y) for _, y in NEAR[1][0] for z in LATE_Z for x in LATE_X]
    rows = np.array([(z * NX + x) * NY + y for z, x, y in sent])
    return (rows[:, None] == np.arange(len(sent))[None, :]).astype(np.float32)


def line_of(ref, column):
    return ref[0:1, column * LANES : (column + 1) * LANES]


def product_kernel(
    eps_occ_ref, order_ref, rows_ref, other_ref, own_hbm, occ_hbm, tiles_hbm,
    out_ref, scalars_ref, own_ref, occ_ref, tiles_ref, sems,
):
    occ_copy = pltpu.make_async_copy(occ_hbm, occ_ref, sems.at[0])
    tiles_copy = pltpu.make_async_copy(tiles_hbm, tiles_ref, sems.at[1])
    own_copy = pltpu.make_async_copy(own_hbm, own_ref, sems.at[2])
    for copy in (occ_copy, tiles_copy, own_copy):
        copy.start()
    core = lax.axis_index("c")
    groups, share, _ = out_ref.shape
    width = own_ref.shape[1]
    rows = rows_ref[...].reshape(groups * share, -1)
    rows = jnp.dot(order_ref[core], rows, preferred_element_type=jnp.float32).astype(jnp.bfloat16)

    def multiply(panel_ref, place):
        part = jnp.dot(rows, panel_ref[...], preferred_element_type=jnp.float32)
        columns = pl.ds(pl.multiple_of(place * width, width), width)
        out_ref[:, :, columns] = part.astype(jnp.bfloat16).reshape(groups, share, width)

    multiply(other_ref, 1 - core)
    occ_copy.wait()
    tiles_copy.wait()
    row_scalars(occ_ref, tiles_ref, eps_occ_ref, scalars_ref)
    own_copy.wait()
    multiply(own_ref, core)


def full_line(ref, start):
    size = min(LANES, ref.shape[0] - start)
    line = ref[start : start + size].reshape(1, size)
    if size == LANES:
        return line
    return jnp.concatenate([line, jnp.zeros((1, LANES - size), line.dtype)], axis=1)


def row_scalars(occ_ref, tiles_ref, eps_occ_ref, scalars_ref):
    lane = lax.broadcasted_iota(jnp.int32, (1, LANES), 1)
    occ_line = full_line(eps_occ_ref, 0)

    def occupied(orbital):
        return jnp.sum(jnp.where(lane == orbital, occ_line, 0.0), axis=1, keepdims=True)

    occ_sum = occupied(occ_ref[0:1, 0:1]) + occupied(occ_ref[0:1, 1:2])
    scalars_ref[0:1, :] = jnp.broadcast_to(occ_sum, (1, LANES))
    for pair in range(tiles_ref.shape[0]):
        for which in range(2):
            tile = tiles_ref[pair : pair + 1, which : which + 1].astype(jnp.float32)
            at = 1 + 2 * pair + which
            scalars_ref[at : at + 1, :] = jnp.broadcast_to(tile, (1, LANES))


def denominators(scalars_ref, eps_vir_ref, tile_pairs):
    tile_rows = TW * TW // LANES
    lane = lax.broadcasted_iota(jnp.int32, (1, LANES), 1)
    grid_lane = lax.broadcasted_iota(jnp.int32, (tile_rows, LANES), 1)
    grid_row = lax.broadcasted_iota(jnp.int32, (tile_rows, LANES), 0)
    lines = [full_line(eps_vir_ref, start) for start in range(0, eps_vir_ref.shape[0], LANES)]

    def orbitals(at):
        tile = scalars_ref[at : at + 1, :].astype(jnp.int32)
        picked = lines[0]
        for at in range(1, len(lines)):
            picked = jnp.where(tile >> 1 == at, lines[at], picked)
        return jnp.where(tile & 1 == 1, pltpu.roll(picked, TW, 1), picked)

    occ_sum = scalars_ref[0:1, :]
    blocks = []
    for pair in range(tile_pairs):
        first = jnp.broadcast_to(orbitals(1 + 2 * pair), (tile_rows, LANES))
        second = orbitals(2 + 2 * pair)
        second = jnp.where(lane < TW, second, pltpu.roll(second, TW, 1))
        even = jnp.sum(jnp.where(grid_lane == 2 * grid_row, first, 0.0), axis=1, keepdims=True)
        odd = jnp.sum(jnp.where(grid_lane == 2 * grid_row + 1, first, 0.0), axis=1, keepdims=True)
        blocks.append(jnp.where(grid_lane < TW, even, odd) + second - occ_sum)
    return blocks


def finish_kernel(scalars_ref, eps_vir_ref, driver_ref, parts_ref, residual_ref, increment_ref, wide, line):
    for column in range(driver_ref.shape[1] // LANES):
        wide[column : column + 1, :] = line_of(driver_ref, column).astype(jnp.float32)
    denominator = jnp.concatenate(denominators(scalars_ref, eps_vir_ref, wide.shape[0] * LANES // TW**2), axis=0)
    for at in range(wide.shape[0] // 8):
        places = [place for place, (z, _, _) in enumerate(FAR[0][0]) if z == at]
        ladder = sum(parts_ref[place].astype(jnp.float32) for place in places)
        residual = (wide[at * 8 : at * 8 + 8, :] + ladder).astype(jnp.bfloat16).astype(jnp.float32)
        increment = residual / denominator[at * 8 : at * 8 + 8, :]
        for row in range(8):
            columns = slice((at * 8 + row) * LANES, (at * 8 + row + 1) * LANES)
            line[0:1, columns] = residual[row : row + 1, :]
            increment_ref[0:1, columns] = increment[row : row + 1, :]
    residual_ref[...] = line[...].astype(jnp.bfloat16)


def per_device(amplitudes, integrals, driver, occ_pairs, ab_tiles, eps_occ, eps_vir):
    other = lax.ppermute(integrals, "c", [(0, 1), (1, 0)])
    rows = lax.all_gather(lax.optimization_barrier(amplitudes[None]), "z", axis=0, tiled=True)
    width = NCORE * integrals.shape[1]
    share = NZ * NYH
    columns = driver.shape[1]
    near, scalars = pl.pallas_call(
        product_kernel,
        out_shape=(
            jax.ShapeDtypeStruct((NX * NYL, share, width), jnp.bfloat16),
            jax.ShapeDtypeStruct((8, LANES), jnp.float32),
        ),
        in_specs=[VMEM_SPEC] * 4 + [pl.BlockSpec(memory_space=pl.ANY)] * 3,
        out_specs=(VMEM_SPEC, VMEM_SPEC),
        scratch_shapes=[
            pltpu.VMEM(integrals.shape, jnp.bfloat16),
            pltpu.VMEM(occ_pairs.shape, jnp.int32),
            pltpu.VMEM(ab_tiles.shape, jnp.int32),
            pltpu.SemaphoreType.DMA((3,)),
        ],
        compiler_params=pltpu.CompilerParams(vmem_limit_bytes=201 * 2**18),
        name="product",
    )(eps_occ, jnp.asarray(np.stack([row_order(core) for core in range(NCORE)]), jnp.bfloat16), rows, other, integrals, occ_pairs, ab_tiles)
    near = lax.all_to_all(near, ("c", "x", "y"), 0, 0, axis_index_groups=NEAR_GROUPS)
    sums = jnp.sum(near.astype(jnp.float32), axis=0).astype(jnp.bfloat16)
    far = lax.all_to_all(
        sums.reshape(share, width // LANES, LANES), ("z", "c", "x", "y"), 0, 0, axis_index_groups=FAR_GROUPS
    )
    return pl.pallas_call(
        finish_kernel,
        out_shape=(
            jax.ShapeDtypeStruct((1, columns), jnp.bfloat16),
            jax.ShapeDtypeStruct((1, columns), jnp.float32),
        ),
        in_specs=[VMEM_SPEC] * 4,
        out_specs=(VMEM_SPEC, VMEM_SPEC),
        scratch_shapes=[
            pltpu.VMEM((columns // LANES, LANES), jnp.float32),
            pltpu.VMEM((1, columns), jnp.float32),
        ],
        compiler_params=pltpu.CompilerParams(vmem_limit_bytes=8 * 2**20),
        name="finish",
    )(scalars, eps_vir, driver, far)


def solution(mesh):
    devices = np.asarray(mesh.devices).reshape(NZ, NCORE, NX, NY)
    fine = Mesh(devices, ("z", "c", "x", "y"))
    pair, integ = ("z", "c"), ("x", "y")
    every = pair + integ
    placed = (P(pair, integ), P(integ, pair), P(every, None), P(every, None), P(), P(), P())
    return jax.shard_map(
        per_device,
        mesh=fine,
        in_specs=placed,
        out_specs=(P(every, None), P(every, None)),
        check_vma=False,
    )
```

```python
import jax
import jax.numpy as jnp
import numpy as np
from jax import lax
from jax.experimental import pallas as pl
from jax.experimental.pallas import tpu as pltpu
from jax.sharding import Mesh, PartitionSpec as P

TW = 64
LANES = 128
NZ, NCORE, NX, NY = 12, 2, 4, 8
VMEM_SPEC = pl.BlockSpec(memory_space=pltpu.VMEM)


def late_first(count):
    return [(at + count // 2) % count for at in range(count)]


LATE_Z, LATE_X, LATE_Y = late_first(NZ), late_first(NX), late_first(NY)
NEAR = (
    [[(x, y + odd) for x in LATE_X for odd in range(2)] for y in range(0, NY, 2)],
    [[(x, (y + 1 - odd) % NY) for x in LATE_X for odd in range(2)] for y in range(1, NY, 2)],
)
FAR = [[(z, x, y + odd) for z in LATE_Z for y in LATE_Y[::2]] for x in range(NX) for odd in range(2)]
NEAR_GROUPS = [[(core * NX + x) * NY + y for x, y in group] for core in range(NCORE) for group in NEAR[core]]
FAR_GROUPS = [[((z * NCORE + core) * NX + x) * NY + y for z, x, y in group] for core in range(NCORE) for group in FAR]


def row_order():
    sent = [(z, x, y + odd) for x, odd in NEAR[0][0] for z in LATE_Z for y in LATE_Y[::2]]
    rows = np.array([(z * NX + x) * NY + y for z, x, y in sent])
    return (rows[:, None] == np.arange(len(sent))[None, :]).astype(np.float32)


def line_of(ref, column):
    return ref[0:1, column * LANES : (column + 1) * LANES]


def product_kernel(
    eps_occ_ref, order_ref, rows_ref, other_ref, own_hbm, occ_hbm, tiles_hbm,
    out_ref, scalars_ref, own_ref, occ_ref, tiles_ref, sems,
):
    occ_copy = pltpu.make_async_copy(occ_hbm, occ_ref, sems.at[0])
    tiles_copy = pltpu.make_async_copy(tiles_hbm, tiles_ref, sems.at[1])
    own_copy = pltpu.make_async_copy(own_hbm, own_ref, sems.at[2])
    for copy in (occ_copy, tiles_copy, own_copy):
        copy.start()
    core = lax.axis_index("c")
    groups, share, _ = out_ref.shape
    width = own_ref.shape[1]
    rows = rows_ref[...].reshape(groups * share, -1)
    rows = jnp.dot(order_ref[...], rows, preferred_element_type=jnp.float32).astype(jnp.bfloat16)

    def multiply(panel_ref, place):
        part = jnp.dot(rows, panel_ref[...], preferred_element_type=jnp.float32)
        columns = pl.ds(pl.multiple_of(place * width, width), width)
        out_ref[:, :, columns] = part.astype(jnp.bfloat16).reshape(groups, share, width)

    multiply(other_ref, 1 - core)
    occ_copy.wait()
    tiles_copy.wait()
    row_scalars(occ_ref, tiles_ref, eps_occ_ref, scalars_ref)
    own_copy.wait()
    multiply(own_ref, core)


def full_line(ref, start):
    size = min(LANES, ref.shape[0] - start)
    line = ref[start : start + size].reshape(1, size)
    if size == LANES:
        return line
    return jnp.concatenate([line, jnp.zeros((1, LANES - size), line.dtype)], axis=1)


def row_scalars(occ_ref, tiles_ref, eps_occ_ref, scalars_ref):
    lane = lax.broadcasted_iota(jnp.int32, (1, LANES), 1)
    occ_line = full_line(eps_occ_ref, 0)

    def occupied(orbital):
        return jnp.sum(jnp.where(lane == orbital, occ_line, 0.0), axis=1, keepdims=True)

    occ_sum = occupied(occ_ref[0:1, 0:1]) + occupied(occ_ref[0:1, 1:2])
    scalars_ref[0:1, :] = jnp.broadcast_to(occ_sum, (1, LANES))
    for pair in range(tiles_ref.shape[0]):
        for which in range(2):
            tile = tiles_ref[pair : pair + 1, which : which + 1].astype(jnp.float32)
            at = 1 + 2 * pair + which
            scalars_ref[at : at + 1, :] = jnp.broadcast_to(tile, (1, LANES))


def denominators(scalars_ref, eps_vir_ref, tile_pairs):
    tile_rows = TW * TW // LANES
    lane = lax.broadcasted_iota(jnp.int32, (1, LANES), 1)
    grid_lane = lax.broadcasted_iota(jnp.int32, (tile_rows, LANES), 1)
    grid_row = lax.broadcasted_iota(jnp.int32, (tile_rows, LANES), 0)
    lines = [full_line(eps_vir_ref, start) for start in range(0, eps_vir_ref.shape[0], LANES)]

    def orbitals(at):
        tile = scalars_ref[at : at + 1, :].astype(jnp.int32)
        picked = lines[0]
        for at in range(1, len(lines)):
            picked = jnp.where(tile >> 1 == at, lines[at], picked)
        return jnp.where(tile & 1 == 1, pltpu.roll(picked, TW, 1), picked)

    occ_sum = scalars_ref[0:1, :]
    blocks = []
    for pair in range(tile_pairs):
        first = jnp.broadcast_to(orbitals(1 + 2 * pair), (tile_rows, LANES))
        second = orbitals(2 + 2 * pair)
        second = jnp.where(lane < TW, second, pltpu.roll(second, TW, 1))
        even = jnp.sum(jnp.where(grid_lane == 2 * grid_row, first, 0.0), axis=1, keepdims=True)
        odd = jnp.sum(jnp.where(grid_lane == 2 * grid_row + 1, first, 0.0), axis=1, keepdims=True)
        blocks.append(jnp.where(grid_lane < TW, even, odd) + second - occ_sum)
    return blocks


def finish_kernel(scalars_ref, eps_vir_ref, driver_ref, parts_ref, residual_ref, increment_ref, wide, line):
    for column in range(driver_ref.shape[1] // LANES):
        wide[column : column + 1, :] = line_of(driver_ref, column).astype(jnp.float32)
    denominator = jnp.concatenate(denominators(scalars_ref, eps_vir_ref, wide.shape[0] * LANES // TW**2), axis=0)
    for at in range(wide.shape[0] // 8):
        places = [place for place, (z, _, _) in enumerate(FAR[0]) if z == at]
        ladder = sum(parts_ref[place].astype(jnp.float32) for place in places)
        residual = (wide[at * 8 : at * 8 + 8, :] + ladder).astype(jnp.bfloat16).astype(jnp.float32)
        increment = residual / denominator[at * 8 : at * 8 + 8, :]
        for row in range(8):
            columns = slice((at * 8 + row) * LANES, (at * 8 + row + 1) * LANES)
            line[0:1, columns] = residual[row : row + 1, :]
            increment_ref[0:1, columns] = increment[row : row + 1, :]
    residual_ref[...] = line[...].astype(jnp.bfloat16)


def per_device(amplitudes, integrals, driver, occ_pairs, ab_tiles, eps_occ, eps_vir):
    other = lax.ppermute(integrals, "c", [(0, 1), (1, 0)])
    rows = lax.all_gather(lax.optimization_barrier(amplitudes[None]), "z", axis=0, tiled=True)
    width = NCORE * integrals.shape[1]
    groups, share = len(NEAR[0][0]), len(FAR[0])
    columns = driver.shape[1]
    near, scalars = pl.pallas_call(
        product_kernel,
        out_shape=(
            jax.ShapeDtypeStruct((groups, share, width), jnp.bfloat16),
            jax.ShapeDtypeStruct((8, LANES), jnp.float32),
        ),
        in_specs=[VMEM_SPEC] * 4 + [pl.BlockSpec(memory_space=pl.ANY)] * 3,
        out_specs=(VMEM_SPEC, VMEM_SPEC),
        scratch_shapes=[
            pltpu.VMEM(integrals.shape, jnp.bfloat16),
            pltpu.VMEM(occ_pairs.shape, jnp.int32),
            pltpu.VMEM(ab_tiles.shape, jnp.int32),
            pltpu.SemaphoreType.DMA((3,)),
        ],
        compiler_params=pltpu.CompilerParams(vmem_limit_bytes=51 * 2**20),
        name="product",
    )(eps_occ, jnp.asarray(row_order(), jnp.bfloat16), rows, other, integrals, occ_pairs, ab_tiles)
    near = lax.all_to_all(near, ("c", "x", "y"), 0, 0, axis_index_groups=NEAR_GROUPS)
    sums = jnp.sum(near.astype(jnp.float32), axis=0).astype(jnp.bfloat16)
    far = lax.all_to_all(
        sums.reshape(share, width // LANES, LANES), ("z", "c", "x", "y"), 0, 0, axis_index_groups=FAR_GROUPS
    )
    return pl.pallas_call(
        finish_kernel,
        out_shape=(
            jax.ShapeDtypeStruct((1, columns), jnp.bfloat16),
            jax.ShapeDtypeStruct((1, columns), jnp.float32),
        ),
        in_specs=[VMEM_SPEC] * 4,
        out_specs=(VMEM_SPEC, VMEM_SPEC),
        scratch_shapes=[
            pltpu.VMEM((columns // LANES, LANES), jnp.float32),
            pltpu.VMEM((1, columns), jnp.float32),
        ],
        compiler_params=pltpu.CompilerParams(vmem_limit_bytes=8 * 2**20),
        name="finish",
    )(scalars, eps_vir, driver, far)


def solution(mesh):
    devices = np.asarray(mesh.devices).reshape(NZ, NCORE, NX, NY)
    fine = Mesh(devices, ("z", "c", "x", "y"))
    pair, integ = ("z", "c"), ("x", "y")
    every = pair + integ
    placed = (P(pair, integ), P(integ, pair), P(every, None), P(every, None), P(), P(), P())
    return jax.shard_map(
        per_device,
        mesh=fine,
        in_specs=placed,
        out_specs=(P(every, None), P(every, None)),
        check_vma=False,
    )
```

```python
import jax
import jax.numpy as jnp
import numpy as np
from jax import lax
from jax.experimental import pallas as pl
from jax.experimental.pallas import tpu as pltpu
from jax.sharding import Mesh, PartitionSpec as P

TW = 64
LANES = 128
NZ, NCORE, NX, NYH, NYL = 12, 2, 4, 4, 2
VMEM_SPEC = pl.BlockSpec(memory_space=pltpu.VMEM)


NEAR = [((x + 2) % NX, yl) for x in range(NX) for yl in range(NYL)]
Z_ORDER = (6, 0, 1, 2, 11, 3, 10, 4, 9, 5, 8, 7)
FAR = [(z, (yh + NYH // 2) % NYH) for z in Z_ORDER for yh in range(NYH)]
NEAR_GROUP = [[x * NYL + yl for x, yl in NEAR]]
FAR_GROUP = [[z * NYH + yh for z, yh in FAR]]


def row_order():
    count = NZ * NX * NYH * NYL
    rows = np.array([((z * NX + x) * NYH + yh) * NYL + yl for x, yl in NEAR for z, yh in FAR])
    return (rows[:, None] == np.arange(count)[None, :]).astype(np.float32)


def line_of(ref, column):
    return ref[0:1, column * LANES : (column + 1) * LANES]


def product_kernel(
    eps_occ_ref, order_ref, rows_ref, other_ref, own_hbm, occ_hbm, tiles_hbm,
    out_ref, scalars_ref, own_ref, occ_ref, tiles_ref, sems,
):
    occ_copy = pltpu.make_async_copy(occ_hbm, occ_ref, sems.at[0])
    tiles_copy = pltpu.make_async_copy(tiles_hbm, tiles_ref, sems.at[1])
    own_copy = pltpu.make_async_copy(own_hbm, own_ref, sems.at[2])
    for copy in (occ_copy, tiles_copy, own_copy):
        copy.start()
    core = lax.axis_index("c")
    groups, share, _ = out_ref.shape
    width = own_ref.shape[1]
    rows = rows_ref[...].reshape(groups * share, -1)
    rows = jnp.dot(order_ref[...], rows, preferred_element_type=jnp.float32).astype(jnp.bfloat16)

    def multiply(panel_ref, place):
        part = jnp.dot(rows, panel_ref[...], preferred_element_type=jnp.float32)
        columns = pl.ds(pl.multiple_of(place * width, width), width)
        out_ref[:, :, columns] = part.astype(jnp.bfloat16).reshape(groups, share, width)

    multiply(other_ref, 1 - core)
    occ_copy.wait()
    tiles_copy.wait()
    row_scalars(occ_ref, tiles_ref, eps_occ_ref, scalars_ref)
    own_copy.wait()
    multiply(own_ref, core)


def full_line(ref, start):
    size = min(LANES, ref.shape[0] - start)
    line = ref[start : start + size].reshape(1, size)
    if size == LANES:
        return line
    return jnp.concatenate([line, jnp.zeros((1, LANES - size), line.dtype)], axis=1)


def row_scalars(occ_ref, tiles_ref, eps_occ_ref, scalars_ref):
    lane = lax.broadcasted_iota(jnp.int32, (1, LANES), 1)
    occ_line = full_line(eps_occ_ref, 0)

    def occupied(orbital):
        return jnp.sum(jnp.where(lane == orbital, occ_line, 0.0), axis=1, keepdims=True)

    occ_sum = occupied(occ_ref[0:1, 0:1]) + occupied(occ_ref[0:1, 1:2])
    scalars_ref[0:1, :] = jnp.broadcast_to(occ_sum, (1, LANES))
    for pair in range(tiles_ref.shape[0]):
        for which in range(2):
            tile = tiles_ref[pair : pair + 1, which : which + 1].astype(jnp.float32)
            at = 1 + 2 * pair + which
            scalars_ref[at : at + 1, :] = jnp.broadcast_to(tile, (1, LANES))


def denominators(scalars_ref, eps_vir_ref, tile_pairs):
    tile_rows = TW * TW // LANES
    lane = lax.broadcasted_iota(jnp.int32, (1, LANES), 1)
    grid_lane = lax.broadcasted_iota(jnp.int32, (tile_rows, LANES), 1)
    grid_row = lax.broadcasted_iota(jnp.int32, (tile_rows, LANES), 0)
    lines = [full_line(eps_vir_ref, start) for start in range(0, eps_vir_ref.shape[0], LANES)]

    def orbitals(at):
        tile = scalars_ref[at : at + 1, :].astype(jnp.int32)
        picked = lines[0]
        for at in range(1, len(lines)):
            picked = jnp.where(tile >> 1 == at, lines[at], picked)
        return jnp.where(tile & 1 == 1, pltpu.roll(picked, TW, 1), picked)

    occ_sum = scalars_ref[0:1, :]
    blocks = []
    for pair in range(tile_pairs):
        first = jnp.broadcast_to(orbitals(1 + 2 * pair), (tile_rows, LANES))
        second = orbitals(2 + 2 * pair)
        second = jnp.where(lane < TW, second, pltpu.roll(second, TW, 1))
        even = jnp.sum(jnp.where(grid_lane == 2 * grid_row, first, 0.0), axis=1, keepdims=True)
        odd = jnp.sum(jnp.where(grid_lane == 2 * grid_row + 1, first, 0.0), axis=1, keepdims=True)
        blocks.append(jnp.where(grid_lane < TW, even, odd) + second - occ_sum)
    return blocks


def finish_kernel(scalars_ref, eps_vir_ref, driver_ref, parts_ref, residual_ref, increment_ref, wide, line):
    for column in range(driver_ref.shape[1] // LANES):
        wide[column : column + 1, :] = line_of(driver_ref, column).astype(jnp.float32)
    denominator = jnp.concatenate(denominators(scalars_ref, eps_vir_ref, wide.shape[0] * LANES // TW**2), axis=0)
    for at in range(wide.shape[0] // 8):
        places = [place for place, (z, _) in enumerate(FAR) if z == at]
        ladder = sum(parts_ref[place].astype(jnp.float32) for place in places)
        residual = (wide[at * 8 : at * 8 + 8, :] + ladder).astype(jnp.bfloat16).astype(jnp.float32)
        increment = residual / denominator[at * 8 : at * 8 + 8, :]
        for row in range(8):
            columns = slice((at * 8 + row) * LANES, (at * 8 + row + 1) * LANES)
            line[0:1, columns] = residual[row : row + 1, :]
            increment_ref[0:1, columns] = increment[row : row + 1, :]
    residual_ref[...] = line[...].astype(jnp.bfloat16)


def per_device(amplitudes, integrals, driver, occ_pairs, ab_tiles, eps_occ, eps_vir):
    other = lax.ppermute(integrals, "c", [(0, 1), (1, 0)])
    rows = lax.all_gather(lax.optimization_barrier(amplitudes[None]), "z", axis=0, tiled=True)
    width = NCORE * integrals.shape[1]
    share = NZ * NYH
    columns = driver.shape[1]
    by_x, scalars = pl.pallas_call(
        product_kernel,
        out_shape=(
            jax.ShapeDtypeStruct((NX * NYL, share, width), jnp.bfloat16),
            jax.ShapeDtypeStruct((8, LANES), jnp.float32),
        ),
        in_specs=[VMEM_SPEC] * 4 + [pl.BlockSpec(memory_space=pl.ANY)] * 3,
        out_specs=(VMEM_SPEC, VMEM_SPEC),
        scratch_shapes=[
            pltpu.VMEM(integrals.shape, jnp.bfloat16),
            pltpu.VMEM(occ_pairs.shape, jnp.int32),
            pltpu.VMEM(ab_tiles.shape, jnp.int32),
            pltpu.SemaphoreType.DMA((3,)),
        ],
        compiler_params=pltpu.CompilerParams(vmem_limit_bytes=51 * 2**20),
        name="product",
    )(eps_occ, jnp.asarray(row_order(), jnp.bfloat16), rows, other, integrals, occ_pairs, ab_tiles)
    by_x = lax.all_to_all(by_x, ("x", "yl"), 0, 0, axis_index_groups=NEAR_GROUP)
    over_x = jnp.sum(by_x.astype(jnp.float32), axis=0).astype(jnp.bfloat16)
    by_z = lax.all_to_all(
        over_x.reshape(share, width // LANES, LANES), ("z", "yh"), 0, 0, axis_index_groups=FAR_GROUP
    )
    return pl.pallas_call(
        finish_kernel,
        out_shape=(
            jax.ShapeDtypeStruct((1, columns), jnp.bfloat16),
            jax.ShapeDtypeStruct((1, columns), jnp.float32),
        ),
        in_specs=[VMEM_SPEC] * 4,
        out_specs=(VMEM_SPEC, VMEM_SPEC),
        scratch_shapes=[
            pltpu.VMEM((columns // LANES, LANES), jnp.float32),
            pltpu.VMEM((1, columns), jnp.float32),
        ],
        compiler_params=pltpu.CompilerParams(vmem_limit_bytes=8 * 2**20),
        name="finish",
    )(scalars, eps_vir, driver, by_z)


def solution(mesh):
    devices = np.asarray(mesh.devices).reshape(NZ, NCORE, NX, NYH, NYL)
    fine = Mesh(devices, ("z", "c", "x", "yh", "yl"))
    pair, integ = ("z", "c"), ("x", "yh", "yl")
    every = pair + integ
    placed = (P(pair, integ), P(integ, pair), P(every, None), P(every, None), P(), P(), P())
    return jax.shard_map(
        per_device,
        mesh=fine,
        in_specs=placed,
        out_specs=(P(every, None), P(every, None)),
        check_vma=False,
    )
```

```python
import jax
import jax.numpy as jnp
import numpy as np
from jax import lax
from jax.experimental import pallas as pl
from jax.experimental.pallas import tpu as pltpu
from jax.sharding import Mesh, PartitionSpec as P

TW = 64
LANES = 128
NZ, NCORE, NX, NYH, NYL = 12, 2, 4, 4, 2
VMEM_SPEC = pl.BlockSpec(memory_space=pltpu.VMEM)


NEAR = [((x + 2) % NX, yl) for x in range(NX) for yl in reversed(range(NYL))]
Z_ORDER = (6, 0, 1, 2, 11, 3, 10, 4, 9, 5, 8, 7)
FAR = [(z, (yh + NYH // 2) % NYH) for z in Z_ORDER for yh in range(NYH)]
NEAR_GROUP = [[x * NYL + yl for x, yl in NEAR]]
FAR_GROUP = [[z * NYH + yh for z, yh in FAR]]


def row_order():
    count = NZ * NX * NYH * NYL
    rows = np.array([((z * NX + x) * NYH + yh) * NYL + yl for x, yl in NEAR for z, yh in FAR])
    return (rows[:, None] == np.arange(count)[None, :]).astype(np.float32)


def line_of(ref, column):
    return ref[0:1, column * LANES : (column + 1) * LANES]


def product_kernel(
    eps_occ_ref, order_ref, rows_ref, other_ref, own_hbm, occ_hbm, tiles_hbm,
    out_ref, scalars_ref, own_ref, occ_ref, tiles_ref, sems,
):
    occ_copy = pltpu.make_async_copy(occ_hbm, occ_ref, sems.at[0])
    tiles_copy = pltpu.make_async_copy(tiles_hbm, tiles_ref, sems.at[1])
    own_copy = pltpu.make_async_copy(own_hbm, own_ref, sems.at[2])
    for copy in (occ_copy, tiles_copy, own_copy):
        copy.start()
    core = lax.axis_index("c")
    groups, share, _ = out_ref.shape
    width = own_ref.shape[1]
    rows = rows_ref[...].reshape(groups * share, -1)
    rows = jnp.dot(order_ref[...], rows, preferred_element_type=jnp.float32).astype(jnp.bfloat16)

    def multiply(panel_ref, place):
        part = jnp.dot(rows, panel_ref[...], preferred_element_type=jnp.float32)
        columns = pl.ds(pl.multiple_of(place * width, width), width)
        out_ref[:, :, columns] = part.astype(jnp.bfloat16).reshape(groups, share, width)

    multiply(other_ref, 1 - core)
    occ_copy.wait()
    tiles_copy.wait()
    row_scalars(occ_ref, tiles_ref, eps_occ_ref, scalars_ref)
    own_copy.wait()
    multiply(own_ref, core)


def full_line(ref, start):
    size = min(LANES, ref.shape[0] - start)
    line = ref[start : start + size].reshape(1, size)
    if size == LANES:
        return line
    return jnp.concatenate([line, jnp.zeros((1, LANES - size), line.dtype)], axis=1)


def row_scalars(occ_ref, tiles_ref, eps_occ_ref, scalars_ref):
    lane = lax.broadcasted_iota(jnp.int32, (1, LANES), 1)
    occ_line = full_line(eps_occ_ref, 0)

    def occupied(orbital):
        return jnp.sum(jnp.where(lane == orbital, occ_line, 0.0), axis=1, keepdims=True)

    occ_sum = occupied(occ_ref[0:1, 0:1]) + occupied(occ_ref[0:1, 1:2])
    scalars_ref[0:1, :] = jnp.broadcast_to(occ_sum, (1, LANES))
    for pair in range(tiles_ref.shape[0]):
        for which in range(2):
            tile = tiles_ref[pair : pair + 1, which : which + 1].astype(jnp.float32)
            at = 1 + 2 * pair + which
            scalars_ref[at : at + 1, :] = jnp.broadcast_to(tile, (1, LANES))


def denominators(scalars_ref, eps_vir_ref, tile_pairs):
    tile_rows = TW * TW // LANES
    lane = lax.broadcasted_iota(jnp.int32, (1, LANES), 1)
    grid_lane = lax.broadcasted_iota(jnp.int32, (tile_rows, LANES), 1)
    grid_row = lax.broadcasted_iota(jnp.int32, (tile_rows, LANES), 0)
    lines = [full_line(eps_vir_ref, start) for start in range(0, eps_vir_ref.shape[0], LANES)]

    def orbitals(at):
        tile = scalars_ref[at : at + 1, :].astype(jnp.int32)
        picked = lines[0]
        for at in range(1, len(lines)):
            picked = jnp.where(tile >> 1 == at, lines[at], picked)
        return jnp.where(tile & 1 == 1, pltpu.roll(picked, TW, 1), picked)

    occ_sum = scalars_ref[0:1, :]
    blocks = []
    for pair in range(tile_pairs):
        first = jnp.broadcast_to(orbitals(1 + 2 * pair), (tile_rows, LANES))
        second = orbitals(2 + 2 * pair)
        second = jnp.where(lane < TW, second, pltpu.roll(second, TW, 1))
        even = jnp.sum(jnp.where(grid_lane == 2 * grid_row, first, 0.0), axis=1, keepdims=True)
        odd = jnp.sum(jnp.where(grid_lane == 2 * grid_row + 1, first, 0.0), axis=1, keepdims=True)
        blocks.append(jnp.where(grid_lane < TW, even, odd) + second - occ_sum)
    return blocks


def finish_kernel(scalars_ref, eps_vir_ref, driver_ref, parts_ref, residual_ref, increment_ref, wide, line):
    for column in range(driver_ref.shape[1] // LANES):
        wide[column : column + 1, :] = line_of(driver_ref, column).astype(jnp.float32)
    denominator = jnp.concatenate(denominators(scalars_ref, eps_vir_ref, wide.shape[0] * LANES // TW**2), axis=0)
    for at in range(wide.shape[0] // 8):
        places = [place for place, (z, _) in enumerate(FAR) if z == at]
        ladder = sum(parts_ref[place].astype(jnp.float32) for place in places)
        residual = (wide[at * 8 : at * 8 + 8, :] + ladder).astype(jnp.bfloat16).astype(jnp.float32)
        increment = residual / denominator[at * 8 : at * 8 + 8, :]
        for row in range(8):
            columns = slice((at * 8 + row) * LANES, (at * 8 + row + 1) * LANES)
            line[0:1, columns] = residual[row : row + 1, :]
            increment_ref[0:1, columns] = increment[row : row + 1, :]
    residual_ref[...] = line[...].astype(jnp.bfloat16)


def per_device(amplitudes, integrals, driver, occ_pairs, ab_tiles, eps_occ, eps_vir):
    other = lax.ppermute(integrals, "c", [(0, 1), (1, 0)])
    rows = lax.all_gather(lax.optimization_barrier(amplitudes[None]), "z", axis=0, tiled=True)
    width = NCORE * integrals.shape[1]
    share = NZ * NYH
    columns = driver.shape[1]
    by_x, scalars = pl.pallas_call(
        product_kernel,
        out_shape=(
            jax.ShapeDtypeStruct((NX * NYL, share, width), jnp.bfloat16),
            jax.ShapeDtypeStruct((8, LANES), jnp.float32),
        ),
        in_specs=[VMEM_SPEC] * 4 + [pl.BlockSpec(memory_space=pl.ANY)] * 3,
        out_specs=(VMEM_SPEC, VMEM_SPEC),
        scratch_shapes=[
            pltpu.VMEM(integrals.shape, jnp.bfloat16),
            pltpu.VMEM(occ_pairs.shape, jnp.int32),
            pltpu.VMEM(ab_tiles.shape, jnp.int32),
            pltpu.SemaphoreType.DMA((3,)),
        ],
        compiler_params=pltpu.CompilerParams(vmem_limit_bytes=51 * 2**20),
        name="product",
    )(eps_occ, jnp.asarray(row_order(), jnp.bfloat16), rows, other, integrals, occ_pairs, ab_tiles)
    by_x = lax.all_to_all(by_x, ("x", "yl"), 0, 0, axis_index_groups=NEAR_GROUP)
    over_x = jnp.sum(by_x.astype(jnp.float32), axis=0).astype(jnp.bfloat16)
    by_z = lax.all_to_all(
        over_x.reshape(share, width // LANES, LANES), ("z", "yh"), 0, 0, axis_index_groups=FAR_GROUP
    )
    return pl.pallas_call(
        finish_kernel,
        out_shape=(
            jax.ShapeDtypeStruct((1, columns), jnp.bfloat16),
            jax.ShapeDtypeStruct((1, columns), jnp.float32),
        ),
        in_specs=[VMEM_SPEC] * 4,
        out_specs=(VMEM_SPEC, VMEM_SPEC),
        scratch_shapes=[
            pltpu.VMEM((columns // LANES, LANES), jnp.float32),
            pltpu.VMEM((1, columns), jnp.float32),
        ],
        compiler_params=pltpu.CompilerParams(vmem_limit_bytes=8 * 2**20),
        name="finish",
    )(scalars, eps_vir, driver, by_z)


def solution(mesh):
    devices = np.asarray(mesh.devices).reshape(NZ, NCORE, NX, NYH, NYL)
    fine = Mesh(devices, ("z", "c", "x", "yh", "yl"))
    pair, integ = ("z", "c"), ("x", "yh", "yl")
    every = pair + integ
    placed = (P(pair, integ), P(integ, pair), P(every, None), P(every, None), P(), P(), P())
    return jax.shard_map(
        per_device,
        mesh=fine,
        in_specs=placed,
        out_specs=(P(every, None), P(every, None)),
        check_vma=False,
    )
```
